32 devices in a mesh: groups: 1, solve: 32 (over z, y, x, core).
Axes of the slice: x: 2, y: 2, z: 4, core: 2. Of those that a mesh axis runs over, the one named last changes fastest.
Arguments:
- beliefs: bfloat16 [16384, 2652], P(('groups', 'solve')), may hold values from 0.099609375 to 2
- targets: bfloat16 [16384, 2652], P(('groups', 'solve')), may hold values from -3 to 3
- leaf_line: int32 [16384], P(('groups', 'solve')), may hold values from 0 to 31
- turn_card: int32 [16384], P(('groups', 'solve')), may hold values from 0 to 51
- encoder: bfloat16 [2652, 1024], P(None, 'solve'), may hold values from -0.125 to 0.125
- value_head: bfloat16 [1024, 2652], P('solve'), may hold values from -0.1875 to 0.1875
- regrets: float32 [32, 1326], P(('groups', 'solve')), may hold values from -1.5 to 1.5
Outputs:
- new_regrets: float32 [32, 1326], P(('groups', 'solve'))
- line_values: float32 [32, 2652], P(('groups', 'solve'))
- head_grad: float32 [1024, 2652], P(('groups', 'solve'))
The draws below stay inside these ranges and needn't reach their ends.
All inputs are finite; a program needn't handle non-finite values.
Results may differ from the reference program's by a relative error of at most 0.004.
Values may be sent and summed in bfloat16 or wider, within the bound.
A program may use at most 128 MiB of HBM per device.

```python
import math
import jax
import jax.numpy as jnp
import numpy as np

HANDS = 1326
NBELIEF = 2652
UNITS = 1024
LEAF_DEV = 512
LEAVES = 16384
LINES = 32


def plant(entries, stream_key, low, largest):
    place = [jax.random.randint(jax.random.fold_in(stream_key, axis), (), 0, length) for axis, length in enumerate(entries.shape)]
    widest = entries.shape.index(max(entries.shape))
    next_to = place[:widest] + [(place[widest] + 1) % entries.shape[widest]] + place[widest + 1:]
    return entries.at[tuple(place)].set(low).at[tuple(next_to)].set(largest)


def levels(stream_key, extent, pieces, least, high):
    loudness, own = 1.0, jax.random.fold_in(stream_key, 6)
    for position, blocks in pieces:
        steps = jnp.exp(jax.random.uniform(jax.random.fold_in(own, position), (blocks,), jnp.float32, least / len(pieces), high / len(pieces)))
        loudness = loudness * jnp.repeat(steps, extent[position] // blocks).reshape([-1 if axis == position else 1 for axis in range(len(extent))])
    return loudness


def normal_values(rng, extent, deviation, reach, cuts=(), held_as=jnp.bfloat16):
    result = jax.random.normal(rng, extent, jnp.float32) * deviation
    if len(cuts) > 0:
        result = levels(rng, extent, cuts, -0.22, 0.18) * result
    return jnp.clip(result, min=-reach, max=reach).astype(held_as)


def setup_inputs(seed: int = 0, part: int = 0) -> dict:
    seeds = jax.random.split(jax.random.key(seed), 8)
    own_keys = jax.random.split(jax.random.fold_in(seeds[7], part), 8)
    return {
        "beliefs": jnp.clip(jnp.exp(math.log(2.0) - 2.9996462 * jax.random.uniform(own_keys[0], (LEAVES, NBELIEF), jnp.float32) ** levels(own_keys[0], (LEAVES, NBELIEF), ((0, 32),), -0.2, 0.2)), 0.099609375, 2.0).astype(jnp.bfloat16),
        "targets": normal_values(own_keys[1], (LEAVES, NBELIEF), 0.5, 3.0, ((0, 32),)),
        "leaf_line": plant(jax.random.randint(own_keys[2], (LEAVES,), 0, LINES), jax.random.fold_in(own_keys[2], 1), 0, LINES - 1).astype(jnp.int32),
        "turn_card": plant(jax.random.randint(own_keys[3], (LEAVES,), 0, 52), jax.random.fold_in(own_keys[3], 1), 0, 51).astype(jnp.int32),
        "encoder": normal_values(seeds[4], (NBELIEF, UNITS), NBELIEF ** -0.5, 0.125, ((1, 32),)),
        "value_head": normal_values(seeds[5], (UNITS, NBELIEF), UNITS ** -0.5, 0.1875, ((0, 32),)),
        "regrets": normal_values(own_keys[6], (LINES, HANDS), 0.2, 1.5, ((0, 32),), jnp.float32),
    }


open_turns = 45.0
regret_floor = 0.05


def blocker_table(hand_count):
    blockers = np.zeros((52, hand_count), np.float32)
    column = 0
    for low_card in range(52):
        for high_card in range(low_card + 1, 52):
            if column < hand_count:
                blockers[low_card, column] = 1.0
                blockers[high_card, column] = 1.0
            column = column + 1
    return blockers


def reference(beliefs, targets, leaf_line, turn_card, encoder, value_head, regrets):
    hidden = jax.nn.silu(jnp.dot(beliefs, encoder, preferred_element_type=jnp.float32)).astype(jnp.bfloat16)
    output = jnp.dot(hidden, value_head, preferred_element_type=jnp.float32)
    errors = ((output - targets.astype(jnp.float32)) / LEAF_DEV).astype(jnp.bfloat16)
    head_grad = jnp.dot(hidden.T, errors, preferred_element_type=jnp.float32)
    leaf_value = output.astype(jnp.bfloat16).astype(jnp.float32)
    blocked = jnp.asarray(blocker_table(HANDS), dtype=jnp.float32)[turn_card]
    open_share = (1.0 - blocked) / open_turns
    weighted = leaf_value * jnp.concatenate([open_share, open_share], 1)
    line_values = jax.ops.segment_sum(weighted, leaf_line, num_segments=LINES)
    positive = jnp.maximum(regrets, 0.0) + regret_floor
    root_value = jnp.sum(positive * line_values[:, :HANDS], 0) / jnp.sum(positive, 0)
    new_regrets = regrets + line_values[:, :HANDS] - root_value[None, :]
    return new_regrets, line_values, head_grad
```

```python
import functools

import jax
import jax.numpy as jnp
import numpy as np
from jax import lax
from jax.experimental import pallas as pl
from jax.experimental.pallas import tpu as pltpu
from jax.sharding import PartitionSpec as P

open_turns = 45.0
regret_floor = 0.05
MESH = pl.DeviceIdType.MESH
F32, BF16 = jnp.float32, jnp.bfloat16
NUM_AT, MSG = 2688, 4096


def blocker_table(hand_count, rows=52):
    blockers = np.zeros((rows, hand_count), np.float32)
    column = 0
    for low_card in range(52):
        for high_card in range(low_card + 1, 52):
            blockers[low_card, column] = 1.0
            blockers[high_card, column] = 1.0
            column = column + 1
    return blockers


def step_kernel(
    nz, hands,
    beliefs, targets, line, card, enc, head, regrets, blockers,
    new_regrets, line_values, head_grad,
    w1, w2, opened, leaf, errors, hidden, hidden_t, partial,
    sib_send, sib_recv, diag_send, diag_recv, xy_send, xy_recv, z_send, z_recv,
    lines_part, msg, msg_in, all_regrets,
    ag_s, ag_r, rs_s, rs_r, reg_s, reg_r, msg_s, msg_r,
):
    n = nz * 8
    rows = enc.shape[0]
    half = rows // 2
    plane = rows * 8
    leaves, width = beliefs.shape
    me = lax.axis_index("solve")
    c = lax.rem(me, 2)
    x = lax.rem(me // 2, 2)
    y = lax.rem(me // 4, 2)
    z = me // 8

    def dev(zz, yy, xx, cc):
        return zz * 8 + yy * 4 + xx * 2 + cc

    def zat(dz):
        return lax.rem(z + dz, nz)

    sib, xn, yn = dev(z, y, x, 1 - c), dev(z, y, 1 - x, c), dev(z, 1 - y, x, c)

    def block(d, start=0, count=rows):
        return pl.ds(pl.multiple_of(d * rows + start, 16), count)

    def remote(src, dst, ss, rs, to):
        return pltpu.make_async_remote_copy(
            src_ref=src, dst_ref=dst, send_sem=ss, recv_sem=rs,
            device_id={"solve": to}, device_id_type=MESH,
        )

    barrier = pltpu.get_barrier_semaphore()

    def greet(i, _):
        pl.semaphore_signal(
            barrier, inc=1, device_id={"solve": lax.rem(me + i, n)}, device_id_type=MESH
        )
        return _

    lax.fori_loop(1, n, greet, 0)
    pl.semaphore_wait(barrier, n - 1)

    started = []
    used = [0, 0]

    def gather_send(k, src_dev, to, part=None, own=None):
        w = (w1, w2)[k]
        span = (0, rows) if part is None else (part * half, half)
        place = w.at[block(src_dev, *span)]
        slot = used[k]
        used[k] += 1
        rsem = ag_r.at[k, src_dev] if part != 1 else ag_r.at[k, n + src_dev // 8]
        cp = remote(place if own is None else own, place, ag_s.at[k, slot], rsem, to)
        cp.start()
        started.append(cp)

    def gather_wait(k, src_dev, part=None):
        w = (w1, w2)[k]
        span = (0, rows) if part is None else (part * half, half)
        place = w.at[block(src_dev, *span)]
        rsem = ag_r.at[k, src_dev] if part != 1 else ag_r.at[k, n + src_dev // 8]
        remote(place, place, ag_s.at[k, 0], rsem, sib).wait_recv()

    for k, own in ((0, enc), (1, head)):
        for dz in (1, nz - 1, 2):
            gather_send(k, me, dev(zat(dz), y, x, c), own=own)
        for to in (xn, yn, sib):
            gather_send(k, me, to, own=own)

    all_regrets[me] = regrets[...]

    def send_regrets(i, _):
        remote(
            all_regrets.at[me], all_regrets.at[me], reg_s, reg_r, lax.rem(me + i, n)
        ).start()
        return _

    lax.fori_loop(1, n, send_regrets, 0)
    w1[block(me)] = enc[...]
    w2[block(me)] = head[...]

    def forward_column(k, dz):
        src = dev(zat(dz), y, x, c)
        gather_wait(k, src)
        for to in (xn, yn, sib):
            gather_send(k, src, to)

    def forward_plane(k, dz):
        src = dev(zat(dz), y, 1 - x, c)
        gather_wait(k, src)
        gather_send(k, src, yn, part=0)
        gather_send(k, src, sib)
        src = dev(zat(dz), 1 - y, x, c)
        gather_wait(k, src)
        gather_send(k, src, xn, part=1)
        gather_send(k, src, sib)

    def forward_diagonal(k, dz):
        src = dev(zat(dz), 1 - y, 1 - x, c)
        gather_wait(k, src, 0)
        gather_wait(k, src, 1)
        gather_send(k, src, sib)

    def wait_sibling(k, dz):
        for yy in (0, 1):
            for xx in (0, 1):
                gather_wait(k, dev(zat(dz), yy, xx, 1 - c))

    for k in (0, 1):
        for dz in (1, nz - 1, 2):
            forward_column(k, dz)
    card_onehot = (
        lax.broadcasted_iota(jnp.int32, (leaves, blockers.shape[0]), 1) == card[...]
    ).astype(F32).astype(BF16)
    for start in range(0, width, 256):
        cols = slice(start, min(start + 256, width))
        opened[:, cols] = (
            1.0 - jnp.dot(card_onehot, blockers[:, cols], preferred_element_type=F32)
        ).astype(BF16)
    for dz in (0, 1, nz - 1, 2):
        forward_plane(0, dz)
    for dz in (0, 1, nz - 1, 2):
        forward_plane(1, dz)
    for dz in (0, 1, nz - 1, 2):
        forward_diagonal(0, dz)

    for dz in (0, 1, nz - 1, 2):
        wait_sibling(0, dz)
        units = pl.ds(pl.multiple_of(zat(dz) * plane, plane), plane)
        pre = lax.dot_general(
            beliefs[...], w1[units, :], (((1,), (1,)), ((), ())), preferred_element_type=F32
        )
        act = pre / (1.0 + jnp.exp(-pre))
        hidden[:, units] = act.astype(BF16)
        hidden_t[units, :] = act.T.astype(BF16)
        forward_diagonal(1, dz)
    for dz in (0, 1, nz - 1, 2):
        wait_sibling(1, dz)

    def output_columns(cols):
        out = jnp.dot(hidden[...], w2[:, cols], preferred_element_type=F32)
        errors[:, cols] = ((out - targets[:, cols].astype(F32)) * (1.0 / leaves)).astype(BF16)
        leaf[:, cols] = out.astype(BF16)

    full = width // 256

    def output_step(j, _):
        output_columns(pl.ds(pl.multiple_of(j * 256, 256), 256))
        return _

    lax.fori_loop(0, full, output_step, 0)
    if full * 256 < width:
        output_columns(slice(full * 256, width))

    order = (1, nz - 1, 2, 0)
    pend = {}
    rs_used = [0]

    def reduce_send(name, src, dst, to):
        slot = rs_used[0]
        rs_used[0] += 1
        cp = remote(src, dst, rs_s.at[slot], rs_r.at[slot], to)
        cp.start()
        started.append(cp)
        pend[name] = cp

    def in_plane(yy, xx, cc):
        return pl.ds(pl.multiple_of((yy * 4 + xx * 2 + cc) * rows, rows), rows)

    rel = ((y, x), (y, 1 - x), (1 - y, x), (1 - y, 1 - x))

    def compute(p):
        units = pl.ds(pl.multiple_of(zat(order[p]) * plane, plane), plane)
        partial[p] = jnp.dot(hidden_t[units, :], errors[...], preferred_element_type=F32)
        for r in (3, 1, 2, 0):
            yy, xx = rel[r]
            sib_send[p, r] = partial[p, in_plane(yy, xx, 1 - c)].astype(BF16)
            reduce_send(("s", p, r), sib_send.at[p, r], sib_recv.at[p, r], sib)

    def chip_sum(p, r, lo=0, count=rows):
        yy, xx = rel[r]
        base = (yy * 4 + xx * 2 + c) * rows + lo
        own = partial[p, pl.ds(pl.multiple_of(base, 16), count)]
        return own + sib_recv[p, r, lo:lo + count].astype(F32)

    def stage_diagonal(p):
        pend["s", p, 3].wait_recv()
        diag_send[p] = chip_sum(p, 3).astype(BF16)
        reduce_send(("a", p), diag_send.at[p, pl.ds(0, half)], diag_recv.at[p, pl.ds(0, half)], yn)
        reduce_send(("b", p), diag_send.at[p, pl.ds(half, half)], diag_recv.at[p, pl.ds(half, half)], xn)

    def stage_neighbours(p):
        pend["s", p, 1].wait_recv()
        pend["a", p].wait_recv()
        xy_send[p, 0, :half] = (chip_sum(p, 1, 0, half) + diag_recv[p, :half].astype(F32)).astype(BF16)
        xy_send[p, 0, half:] = chip_sum(p, 1, half, half).astype(BF16)
        reduce_send(("x", p), xy_send.at[p, 0], xy_recv.at[p, 0], xn)
        pend["s", p, 2].wait_recv()
        pend["b", p].wait_recv()
        xy_send[p, 1, :half] = chip_sum(p, 2, 0, half).astype(BF16)
        xy_send[p, 1, half:] = (chip_sum(p, 2, half, half) + diag_recv[p, half:].astype(F32)).astype(BF16)
        reduce_send(("y", p), xy_send.at[p, 1], xy_recv.at[p, 1], yn)

    def column_sum(p):
        pend["s", p, 0].wait_recv()
        pend["x", p].wait_recv()
        pend["y", p].wait_recv()
        return chip_sum(p, 0) + xy_recv[p, 0].astype(F32) + xy_recv[p, 1].astype(F32)

    def stage_column(p):
        z_send[p] = column_sum(p).astype(BF16)
        reduce_send(("z", p), z_send.at[p], z_recv.at[p], dev(zat(order[p]), y, x, c))

    def line_messages():
        remote(all_regrets.at[pl.ds(0, n - 1)], all_regrets.at[pl.ds(0, n - 1)], reg_s, reg_r, sib).wait_recv()
        onehot = (
            lax.broadcasted_iota(jnp.int32, (n, leaves), 0) == line[...]
        ).astype(F32).astype(BF16)
        for start in range(0, width, 512):
            cols = slice(start, min(start + 512, width))
            masked = (leaf[:, cols].astype(F32) * opened[:, cols].astype(F32)).astype(BF16)
            lines_part[:, cols] = jnp.dot(onehot, masked, preferred_element_type=F32) / open_turns
        numer = jnp.zeros((1, hands), F32)
        for l in range(n):
            row = lines_part[l:l + 1, :]
            msg[l, :, 0:width] = row
            numer += (jnp.maximum(all_regrets[l], 0.0) + regret_floor) * row[:, :hands]
        for l in range(n):
            msg[l, :, NUM_AT:NUM_AT + hands] = numer
        msg_in[me] = msg[me]

        def send(i, _):
            to = lax.rem(me + i, n)
            remote(msg.at[to], msg_in.at[me], msg_s, msg_r, to).start()
            return _

        lax.fori_loop(1, n, send, 0)

    compute(0)
    compute(1)
    stage_diagonal(0)
    compute(2)
    stage_diagonal(1)
    stage_neighbours(0)
    compute(3)
    stage_diagonal(2)
    stage_neighbours(1)
    stage_diagonal(3)
    stage_column(0)
    line_messages()
    stage_neighbours(2)
    stage_column(1)
    stage_neighbours(3)
    stage_column(2)

    remote(msg_in.at[pl.ds(0, n - 1)], msg_in.at[pl.ds(0, n - 1)], msg_s, msg_r, sib).wait_recv()
    total = jnp.zeros((1, MSG), F32)
    denominator = jnp.zeros((1, hands), F32)
    for l in range(n):
        total += msg_in[l]
        denominator += jnp.maximum(all_regrets[l], 0.0) + regret_floor
    line_values[...] = total[:, :width]
    root = total[:, NUM_AT:NUM_AT + hands] / denominator
    new_regrets[...] = regrets[...] + total[:, :hands] - root

    result = column_sum(3)
    for p in range(3):
        pend["z", p].wait_recv()
        result += z_recv[p].astype(F32)
    head_grad[...] = result

    for cp in started:
        cp.wait_send()
    remote(all_regrets.at[pl.ds(0, n - 1)], all_regrets.at[pl.ds(0, n - 1)], reg_s, reg_r, sib).wait_send()
    remote(msg.at[pl.ds(0, n - 1)], msg.at[pl.ds(0, n - 1)], msg_s, msg_r, sib).wait_send()


def fused(nz, beliefs, targets, leaf_line, turn_card, encoder, value_head, regrets):
    n = nz * 8
    leaves, width = beliefs.shape
    hands = regrets.shape[1]
    rows = value_head.shape[0]
    units = rows * n
    table = blocker_table(hands, 64)
    blockers = jnp.asarray(np.concatenate([table, table], 1), dtype=BF16)
    vm = pl.BlockSpec(memory_space=pltpu.VMEM)
    dma = pltpu.SemaphoreType.DMA
    return pl.pallas_call(
        functools.partial(step_kernel, nz, hands),
        out_shape=(
            jax.ShapeDtypeStruct((1, hands), F32),
            jax.ShapeDtypeStruct((1, width), F32),
            jax.ShapeDtypeStruct((rows, width), F32),
        ),
        in_specs=[vm] * 8,
        out_specs=(vm, vm, vm),
        scratch_shapes=[
            pltpu.VMEM((units, width), BF16),
            pltpu.VMEM((units, width), BF16),
            pltpu.VMEM((leaves, width), BF16),
            pltpu.VMEM((leaves, width), BF16),
            pltpu.VMEM((leaves, width), BF16),
            pltpu.VMEM((leaves, units), BF16),
            pltpu.VMEM((units, leaves), BF16),
            pltpu.VMEM((4, rows * 8, width), F32),
            pltpu.VMEM((4, 4, rows, width), BF16),
            pltpu.VMEM((4, 4, rows, width), BF16),
            pltpu.VMEM((4, rows, width), BF16),
            pltpu.VMEM((4, rows, width), BF16),
            pltpu.VMEM((4, 2, rows, width), BF16),
            pltpu.VMEM((4, 2, rows, width), BF16),
            pltpu.VMEM((3, rows, width), BF16),
            pltpu.VMEM((3, rows, width), BF16),
            pltpu.VMEM((n, width), F32),
            pltpu.VMEM((n, 1, MSG), F32),
            pltpu.VMEM((n, 1, MSG), F32),
            pltpu.VMEM((n, 1, hands), F32),
            dma((2, 40)),
            dma((2, n + nz)),
            dma((40,)),
            dma((40,)),
            dma, dma, dma, dma,
        ],
        compiler_params=pltpu.CompilerParams(
            collective_id=0, has_side_effects=True, vmem_limit_bytes=60 * 2**20
        ),
        cost_estimate=pl.CostEstimate(
            flops=6 * leaves * width * units, bytes_accessed=12 * 2**20, transcendentals=leaves * units
        ),
    )(
        beliefs, targets, leaf_line.reshape(1, leaves), turn_card.reshape(leaves, 1),
        encoder.T, value_head, regrets, blockers,
    )


def by_collectives(beliefs, targets, leaf_line, turn_card, encoder, value_head, regrets):
    devices = lax.axis_size("solve")
    leaf_count = beliefs.shape[0]
    hand_count = regrets.shape[1]
    line_count = regrets.shape[0] * devices
    hidden = jax.nn.silu(
        jnp.dot(
            beliefs,
            lax.all_gather(encoder, "solve", axis=1, tiled=True),
            preferred_element_type=F32,
        )
    ).astype(BF16)
    output = jnp.dot(
        hidden,
        lax.all_gather(value_head, "solve", axis=0, tiled=True),
        preferred_element_type=F32,
    )
    errors = ((output - targets.astype(F32)) / leaf_count).astype(BF16)
    head_grad = lax.psum_scatter(
        lax.dot_general(hidden, errors, (((0,), (0,)), ((), ())), preferred_element_type=F32),
        "solve", scatter_dimension=0, tiled=True,
    )
    card_onehot = (turn_card[:, None] == jnp.arange(52, dtype=jnp.int32)[None, :]).astype(BF16)
    blocked = jnp.dot(
        card_onehot, jnp.asarray(blocker_table(hand_count), dtype=BF16), preferred_element_type=F32
    )
    shown = (1.0 - blocked).astype(BF16)
    weighted = output.astype(BF16) * jnp.concatenate([shown, shown], 1)
    line_onehot = (leaf_line[:, None] == jnp.arange(line_count, dtype=jnp.int32)[None, :]).astype(BF16)
    line_values = lax.psum_scatter(
        lax.dot_general(
            line_onehot, weighted, (((0,), (0,)), ((), ())), preferred_element_type=F32
        ) / open_turns,
        "solve", scatter_dimension=0, tiled=True,
    )
    positive = jnp.maximum(regrets, 0.0) + regret_floor
    denominator, numerator = lax.psum(
        (jnp.sum(positive, 0), jnp.sum(positive * line_values[:, :hand_count], 0)), "solve"
    )
    new_regrets = regrets + line_values[:, :hand_count] - (numerator / denominator)[None, :]
    return (new_regrets, line_values, head_grad)


def solution(mesh):
    split = P(("groups", "solve"), None)
    placed = (
        split, split, P(("groups", "solve")), P(("groups", "solve")),
        P(None, "solve"), P("solve", None), split,
    )
    in_tree = mesh.shape["groups"] == 1 and mesh.shape["solve"] == 32
    return jax.shard_map(
        functools.partial(fused, mesh.shape["solve"] // 8) if in_tree else by_collectives,
        mesh=mesh,
        in_specs=placed,
        out_specs=(split, split, split),
        check_vma=False,
    )
```

```python
import functools

import jax
import jax.numpy as jnp
import numpy as np
from jax import lax
from jax.experimental import pallas as pl
from jax.experimental.pallas import tpu as pltpu
from jax.sharding import PartitionSpec as P

open_turns = 45.0
regret_floor = 0.05
MESH = pl.DeviceIdType.MESH
F32, BF16 = jnp.float32, jnp.bfloat16


def blocker_table(hand_count, rows=52):
    blockers = np.zeros((rows, hand_count), np.float32)
    column = 0
    for low_card in range(52):
        for high_card in range(low_card + 1, 52):
            blockers[low_card, column] = 1.0
            blockers[high_card, column] = 1.0
            column = column + 1
    return blockers


def step_kernel(
    nz, hands,
    beliefs, targets, line, card, enc, head, regrets, blockers,
    new_regrets, line_values, head_grad,
    beliefs_t, targets_t, w1, w2, opened, leaf, errors, hidden, hidden_t, partial,
    sib_send, sib_recv, diag_send, diag_recv, xy_send, xy_recv, z_send, z_recv,
    line_tree, line_in, y_send, y_in, lz_send, lz_in, sums, sums_in,
    ag_s, ag_r, rs_s, rs_r, small_s, small_r, load_s,
):
    n = nz * 8
    rows = enc.shape[0]
    half = rows // 2
    plane = rows * 8
    width, leaves = beliefs.shape
    me = lax.axis_index("solve")
    c = lax.rem(me, 2)
    x = lax.rem(me // 2, 2)
    y = lax.rem(me // 4, 2)
    z = me // 8

    def dev(zz, yy, xx, cc):
        return zz * 8 + yy * 4 + xx * 2 + cc

    z_low, z_high = lax.rem(z, 2), z // 2
    zs = (z, z + 1 - 2 * z_low, z + 2 - 4 * z_high, 3 - z)

    sib, xn, yn = dev(z, y, x, 1 - c), dev(z, y, 1 - x, c), dev(z, 1 - y, x, c)

    zp = tuple(dev(zz, y, x, c) for zz in zs)

    def block(d, start=0, count=rows):
        return pl.ds(pl.multiple_of(d * rows + start, 16), count)

    def remote(src, dst, ss, rs, to):
        return pltpu.make_async_remote_copy(
            src_ref=src, dst_ref=dst, send_sem=ss, recv_sem=rs,
            device_id={"solve": to}, device_id_type=MESH,
        )

    loads = [
        pltpu.make_async_copy(beliefs, beliefs_t, load_s.at[0]),
        pltpu.make_async_copy(targets, targets_t, load_s.at[1]),
    ]
    for load in loads:
        load.start()

    barrier = pltpu.get_barrier_semaphore()
    for to in (*zp[1:], xn, yn, sib):
        pl.semaphore_signal(barrier, inc=1, device_id={"solve": to}, device_id_type=MESH)
    pl.semaphore_wait(barrier, 6)

    started = []
    used = [0, 0]

    def gather_send(k, src_dev, to, part=None, own=None):
        w = (w1, w2)[k]
        span = (0, rows) if part is None else (part * half, half)
        place = w.at[block(src_dev, *span)]
        slot = used[k]
        used[k] += 1
        rsem = ag_r.at[k, src_dev] if part != 1 else ag_r.at[k, n + src_dev // 8]
        cp = remote(place if own is None else own, place, ag_s.at[k, slot], rsem, to)
        cp.start()
        started.append(cp)

    def gather_wait(k, src_dev, part=None):
        w = (w1, w2)[k]
        span = (0, rows) if part is None else (part * half, half)
        place = w.at[block(src_dev, *span)]
        rsem = ag_r.at[k, src_dev] if part != 1 else ag_r.at[k, n + src_dev // 8]
        remote(place, place, ag_s.at[k, 0], rsem, sib).wait_recv()

    for k, own in ((0, enc), (1, head)):
        for to in (zp[1], xn, yn, zp[2], zp[3], sib):
            gather_send(k, me, to, own=own)
    w1[block(me)] = enc[...]
    w2[block(me)] = head[...]

    def forward_column(k, q):
        src = dev(zs[q], y, x, c)
        gather_wait(k, src)
        for to in (sib,) if q == 1 else (xn, yn, sib):
            gather_send(k, src, to)

    def forward_plane(k, q):
        src = dev(zs[q], y, 1 - x, c)
        gather_wait(k, src)
        if q == 0:
            gather_send(k, src, zp[1])
        gather_send(k, src, yn, part=0)
        gather_send(k, src, sib)
        src = dev(zs[q], 1 - y, x, c)
        gather_wait(k, src)
        if q == 0:
            gather_send(k, src, zp[1])
        gather_send(k, src, xn, part=1)
        gather_send(k, src, sib)

    def forward_diagonal(k, q):
        src = dev(zs[q], 1 - y, 1 - x, c)
        gather_wait(k, src, 0)
        gather_wait(k, src, 1)
        gather_send(k, src, sib)

    def wait_sibling(k, dz):
        for yy in (0, 1):
            for xx in (0, 1):
                gather_wait(k, dev(zs[dz], yy, xx, 1 - c))

    forward_plane(0, 0)
    for q in (1, 2, 3):
        forward_column(0, q)
    forward_plane(1, 0)
    for q in (1, 2, 3):
        forward_column(1, q)
    for q in (1, 2, 3):
        forward_plane(0, q)
    for q in (1, 2, 3):
        forward_plane(1, q)

    card_onehot = (
        lax.broadcasted_iota(jnp.int32, (blockers.shape[0], leaves), 0) == card[...]
    ).astype(F32).T.astype(BF16)
    for start in range(0, width, 256):
        cols = slice(start, min(start + 256, width))
        opened[:, cols] = (
            1.0 - jnp.dot(card_onehot, blockers[:, cols], preferred_element_type=F32)
        ).astype(BF16)
    for q in range(4):
        forward_diagonal(0, q)

    for load in loads:
        load.wait()
    for q in range(4):
        wait_sibling(0, q)
        units = pl.ds(pl.multiple_of(zs[q] * plane, plane), plane)
        pre = jnp.dot(w1[units, :], beliefs_t[...], preferred_element_type=F32)
        act = pre / (1.0 + jnp.exp(-pre))
        hidden_t[units, :] = act.astype(BF16)
        hidden[:, units] = act.T.astype(BF16)
        forward_diagonal(1, q)
    for start in range(0, width, 256):
        cols = slice(start, min(start + 256, width))
        errors[:, cols] = targets_t[cols, :].astype(F32).T.astype(BF16)
    for q in range(4):
        wait_sibling(1, q)

    def output_columns(cols):
        out = jnp.dot(hidden[...], w2[:, cols], preferred_element_type=F32)
        errors[:, cols] = ((out - errors[:, cols].astype(F32)) * (1.0 / leaves)).astype(BF16)
        leaf[:, cols] = out.astype(BF16)

    full = width // 256

    def output_step(j, _):
        output_columns(pl.ds(pl.multiple_of(j * 256, 256), 256))
        return _

    lax.fori_loop(0, full, output_step, 0)
    if full * 256 < width:
        output_columns(slice(full * 256, width))

    order = (1, 2, 3, 0)
    pend = {}
    rs_used = [0]

    def reduce_send(name, src, dst, to):
        slot = rs_used[0]
        rs_used[0] += 1
        cp = remote(src, dst, rs_s.at[slot], rs_r.at[slot], to)
        cp.start()
        started.append(cp)
        pend[name] = cp

    def in_plane(yy, xx, cc):
        return pl.ds(pl.multiple_of((yy * 4 + xx * 2 + cc) * rows, rows), rows)

    rel = ((y, x), (y, 1 - x), (1 - y, x), (1 - y, 1 - x))

    def compute(p):
        units = pl.ds(pl.multiple_of(zs[order[p]] * plane, plane), plane)
        partial[p] = jnp.dot(hidden_t[units, :], errors[...], preferred_element_type=F32)
        for r in (3, 1, 2, 0):
            yy, xx = rel[r]
            sib_send[p, r] = partial[p, in_plane(yy, xx, 1 - c)].astype(BF16)
            reduce_send(("s", p, r), sib_send.at[p, r], sib_recv.at[p, r], sib)

    def chip_sum(p, r, lo=0, count=rows):
        yy, xx = rel[r]
        base = (yy * 4 + xx * 2 + c) * rows + lo
        own = partial[p, pl.ds(pl.multiple_of(base, 16), count)]
        return own + sib_recv[p, r, lo:lo + count].astype(F32)

    def stage_diagonal(p):
        pend["s", p, 3].wait_recv()
        diag_send[p] = chip_sum(p, 3).astype(BF16)
        reduce_send(("a", p), diag_send.at[p, pl.ds(0, half)], diag_recv.at[p, pl.ds(0, half)], yn)
        reduce_send(("b", p), diag_send.at[p, pl.ds(half, half)], diag_recv.at[p, pl.ds(half, half)], xn)

    def stage_neighbours(p):
        for r, name, to, lo in ((1, "a", xn, 0), (2, "b", yn, half)):
            pend["s", p, r].wait_recv()
            pend[name, p].wait_recv()
            total = chip_sum(p, r)
            there = diag_recv[p, lo:lo + half].astype(F32)
            keep = total[half - lo:half - lo + half]
            mixed = total[lo:lo + half] + there
            if p == 3:
                pend["n", 0, r].wait_recv()
                extra = xy_recv[0, r - 1].astype(F32)
                mixed += extra[lo:lo + half]
                keep += extra[half - lo:half - lo + half]
            xy_send[p, r - 1, lo:lo + half] = mixed.astype(BF16)
            xy_send[p, r - 1, half - lo:half - lo + half] = keep.astype(BF16)
            reduce_send(("n", p, r), xy_send.at[p, r - 1], xy_recv.at[p, r - 1], zp[1] if p == 0 else to)

    def column_sum(p):
        pend["s", p, 0].wait_recv()
        total = chip_sum(p, 0)
        if p > 0:
            for r in (1, 2):
                pend["n", p, r].wait_recv()
                total += xy_recv[p, r - 1].astype(F32)
        return total

    def stage_column(p):
        z_send[p] = column_sum(p).astype(BF16)
        reduce_send(("z", p), z_send.at[p], z_recv.at[p], zp[order[p]])

    small = {}
    small_used = [0]

    def small_send(name, src, dst, to):
        slot = small_used[0]
        small_used[0] += 1
        cp = remote(src, dst, small_s.at[slot], small_r.at[slot], to)
        cp.start()
        started.append(cp)
        small[name] = cp

    def flip(bit, by):
        return bit + by - 2 * bit * by

    def line_terms():
        r = lax.broadcasted_iota(jnp.int32, (n, leaves), 0)
        far = [lax.rem(r // 2 ** b, 2) for b in range(5)]
        owner = (
            16 * flip(z_high, far[1]) + 8 * flip(z_low, far[0])
            + 4 * flip(y, far[2]) + 2 * flip(x, far[3]) + flip(c, far[4])
        )
        onehot = (owner == line[...]).astype(F32).astype(BF16)
        for start in range(0, width, 512):
            cols = slice(start, min(start + 512, width))
            masked = (leaf[:, cols].astype(F32) * opened[:, cols].astype(F32)).astype(BF16)
            line_tree[:, cols] = jnp.dot(onehot, masked, preferred_element_type=F32) / open_turns
        small_send("lc", line_tree.at[pl.ds(16, 16)], line_in.at[pl.ds(16, 16)], sib)

    def line_x():
        small["lc"].wait_recv()
        line_tree[0:16] += line_in[16:32]
        small_send("lx", line_tree.at[pl.ds(8, 8)], line_in.at[pl.ds(8, 8)], xn)

    def line_y():
        small["lx"].wait_recv()
        both = line_tree[0:8] + line_in[8:16]
        line_tree[0:8] = both
        y_send[0:4] = both[4:8]
        small_send("ly", y_send, y_in, yn)

    def line_z():
        small["ly"].wait_recv()
        four = line_tree[0:4] + y_in[0:4]
        line_tree[0:4] = four
        for q in (1, 2, 3):
            lz_send[q - 1] = four[q:q + 1]
            small_send(("lz", q), lz_send.at[q - 1], lz_in.at[q - 1], zp[q])

    positive = jnp.maximum(regrets[...], 0.0) + regret_floor

    def line_done():
        value = line_tree[0:1]
        for q in (1, 2, 3):
            small["lz", q].wait_recv()
            value += lz_in[q - 1]
        line_values[...] = value
        sums[0, 0:1] = positive * value[:, :hands]
        sums[0, 1:2] = positive
        small_send("nc", sums.at[0], sums_in.at[0], sib)

    def sums_step(at, name, following, to):
        small[name].wait_recv()
        sums[at, 0:2] = sums[at - 1, 0:2] + sums_in[at - 1, 0:2]
        for q, dst in enumerate(to):
            small_send((following, q), sums.at[at], sums_in.at[at + q], dst)

    def root_done():
        total = sums[3, 0:2]
        for q in (0, 1, 2):
            small["nz", q].wait_recv()
            total += sums_in[3 + q, 0:2]
        root = total[0:1] / total[1:2]
        new_regrets[...] = regrets[...] + line_values[:, :hands] - root

    y_send[4:8] = jnp.zeros((4, width), F32)
    sums[...] = jnp.zeros_like(sums)
    compute(0)
    compute(1)
    stage_diagonal(0)
    compute(2)
    stage_diagonal(1)
    stage_neighbours(0)
    compute(3)
    stage_diagonal(2)
    stage_neighbours(1)
    stage_column(0)
    stage_diagonal(3)
    line_terms()
    stage_neighbours(2)
    line_x()
    stage_column(1)
    line_y()
    stage_neighbours(3)
    line_z()
    stage_column(2)
    line_done()
    sums_step(1, "nc", "nx", (xn,))
    sums_step(2, ("nx", 0), "ny", (yn,))
    sums_step(3, ("ny", 0), "nz", zp[1:])
    root_done()

    result = column_sum(3)
    for p in range(3):
        pend["z", p].wait_recv()
        result += z_recv[p].astype(F32)
    head_grad[...] = result

    for cp in started:
        cp.wait_send()

def fused(nz, beliefs, targets, leaf_line, turn_card, encoder, value_head, regrets):
    n = nz * 8
    leaves, width = beliefs.shape
    hands = regrets.shape[1]
    rows = value_head.shape[0]
    units = rows * n
    table = blocker_table(hands, 64)
    blockers = jnp.asarray(np.concatenate([table, table], 1), dtype=BF16)
    vm = pl.BlockSpec(memory_space=pltpu.VMEM)
    dma = pltpu.SemaphoreType.DMA
    outs = pl.pallas_call(
        functools.partial(step_kernel, nz, hands),
        out_shape=(
            jax.ShapeDtypeStruct((1, hands), F32),
            jax.ShapeDtypeStruct((1, width), F32),
            jax.ShapeDtypeStruct((rows, width), F32),
        ),
        in_specs=[pl.BlockSpec(memory_space=pl.ANY)] * 2 + [vm] * 6,
        out_specs=(vm, vm, vm),
        scratch_shapes=[
            pltpu.VMEM((width, leaves), BF16),
            pltpu.VMEM((width, leaves), BF16),
            pltpu.VMEM((units, width), BF16),
            pltpu.VMEM((units, width), BF16),
            pltpu.VMEM((leaves, width), BF16),
            pltpu.VMEM((leaves, width), BF16),
            pltpu.VMEM((leaves, width), BF16),
            pltpu.VMEM((leaves, units), BF16),
            pltpu.VMEM((units, leaves), BF16),
            pltpu.VMEM((4, rows * 8, width), F32),
            pltpu.VMEM((4, 4, rows, width), BF16),
            pltpu.VMEM((4, 4, rows, width), BF16),
            pltpu.VMEM((4, rows, width), BF16),
            pltpu.VMEM((4, rows, width), BF16),
            pltpu.VMEM((4, 2, rows, width), BF16),
            pltpu.VMEM((4, 2, rows, width), BF16),
            pltpu.VMEM((3, rows, width), BF16),
            pltpu.VMEM((3, rows, width), BF16),
            pltpu.VMEM((n, width), F32),
            pltpu.VMEM((n, width), F32),
            pltpu.VMEM((8, width), F32),
            pltpu.VMEM((8, width), F32),
            pltpu.VMEM((3, 1, width), F32),
            pltpu.VMEM((3, 1, width), F32),
            pltpu.VMEM((4, 8, hands), F32),
            pltpu.VMEM((6, 8, hands), F32),
            dma((2, 40)),
            dma((2, n + nz)),
            dma((40,)),
            dma((40,)),
            dma((16,)),
            dma((16,)),
            dma((2,)),
        ],
        compiler_params=pltpu.CompilerParams(
            collective_id=0, has_side_effects=True, vmem_limit_bytes=62 * 2**20
        ),
        cost_estimate=pl.CostEstimate(
            flops=6 * leaves * width * units, bytes_accessed=12 * 2**20, transcendentals=leaves * units
        ),
    )(
        beliefs.T, targets.T, leaf_line.reshape(1, leaves), turn_card.reshape(1, leaves),
        encoder.T, value_head, regrets, blockers,
    )
    return pl.pallas_call(
        hand_over, out_shape=tuple(jax.ShapeDtypeStruct(o.shape, o.dtype) for o in outs), in_specs=[vm] * 3, out_specs=(vm, vm, vm)
    )(*outs)


def hand_over(a, b, c, a_out, b_out, c_out):
    a_out[...] = a[...]
    b_out[...] = b[...]
    c_out[...] = c[...]


def by_collectives(beliefs, targets, leaf_line, turn_card, encoder, value_head, regrets):
    devices = lax.axis_size("solve")
    leaf_count = beliefs.shape[0]
    hand_count = regrets.shape[1]
    line_count = regrets.shape[0] * devices
    hidden = jax.nn.silu(
        jnp.dot(
            beliefs,
            lax.all_gather(encoder, "solve", axis=1, tiled=True),
            preferred_element_type=F32,
        )
    ).astype(BF16)
    output = jnp.dot(
        hidden,
        lax.all_gather(value_head, "solve", axis=0, tiled=True),
        preferred_element_type=F32,
    )
    errors = ((output - targets.astype(F32)) / leaf_count).astype(BF16)
    head_grad = lax.psum_scatter(
        lax.dot_general(hidden, errors, (((0,), (0,)), ((), ())), preferred_element_type=F32),
        "solve", scatter_dimension=0, tiled=True,
    )
    card_onehot = (turn_card[:, None] == jnp.arange(52, dtype=jnp.int32)[None, :]).astype(BF16)
    blocked = jnp.dot(
        card_onehot, jnp.asarray(blocker_table(hand_count), dtype=BF16), preferred_element_type=F32
    )
    shown = (1.0 - blocked).astype(BF16)
    weighted = output.astype(BF16) * jnp.concatenate([shown, shown], 1)
    line_onehot = (leaf_line[:, None] == jnp.arange(line_count, dtype=jnp.int32)[None, :]).astype(BF16)
    line_values = lax.psum_scatter(
        lax.dot_general(
            line_onehot, weighted, (((0,), (0,)), ((), ())), preferred_element_type=F32
        ) / open_turns,
        "solve", scatter_dimension=0, tiled=True,
    )
    positive = jnp.maximum(regrets, 0.0) + regret_floor
    denominator, numerator = lax.psum(
        (jnp.sum(positive, 0), jnp.sum(positive * line_values[:, :hand_count], 0)), "solve"
    )
    new_regrets = regrets + line_values[:, :hand_count] - (numerator / denominator)[None, :]
    return (new_regrets, line_values, head_grad)


def solution(mesh):
    split = P(("groups", "solve"), None)
    placed = (
        split, split, P(("groups", "solve")), P(("groups", "solve")),
        P(None, "solve"), P("solve", None), split,
    )
    in_tree = mesh.shape["groups"] == 1 and mesh.shape["solve"] == 32
    return jax.shard_map(
        functools.partial(fused, mesh.shape["solve"] // 8) if in_tree else by_collectives,
        mesh=mesh,
        in_specs=placed,
        out_specs=(split, split, split),
        check_vma=False,
    )
```

```python
import functools

import jax
import jax.numpy as jnp
import numpy as np
from jax import lax
from jax.experimental import pallas as pl
from jax.experimental.pallas import tpu as pltpu
from jax.sharding import PartitionSpec as P

open_turns = 45.0
regret_floor = 0.05
MESH = pl.DeviceIdType.MESH
F32, BF16 = jnp.float32, jnp.bfloat16


def blocker_table(hand_count, rows=52):
    blockers = np.zeros((rows, hand_count), np.float32)
    column = 0
    for low_card in range(52):
        for high_card in range(low_card + 1, 52):
            blockers[low_card, column] = 1.0
            blockers[high_card, column] = 1.0
            column = column + 1
    return blockers


def step_kernel(
    nz, hands,
    beliefs, targets, line, card, enc, head, regrets, blockers,
    new_regrets, line_values, head_grad,
    beliefs_t, targets_t, w1, w2, opened, leaf, errors, hidden, hidden_t, partial,
    sib_send, sib_recv, diag_send, diag_recv, xy_send, xy_recv, z_send, z_recv,
    line_tree, line_in, y_send, y_in, lz_send, lz_in, sums, sums_in,
    ag_s, ag_r, rs_s, rs_r, small_s, small_r, load_s,
):
    n = nz * 8
    rows = enc.shape[0]
    half = rows // 2
    plane = rows * 8
    width, leaves = beliefs.shape
    me = lax.axis_index("solve")
    c = lax.rem(me, 2)
    x = lax.rem(me // 2, 2)
    y = lax.rem(me // 4, 2)
    z = me // 8

    def dev(zz, yy, xx, cc):
        return zz * 8 + yy * 4 + xx * 2 + cc

    z_low, z_high = lax.rem(z, 2), z // 2
    zs = (z, z + 1 - 2 * z_low, z + 2 - 4 * z_high, 3 - z)

    sib, xn, yn = dev(z, y, x, 1 - c), dev(z, y, 1 - x, c), dev(z, 1 - y, x, c)

    zp = tuple(dev(zz, y, x, c) for zz in zs)

    def block(d, start=0, count=rows):
        return pl.ds(pl.multiple_of(d * rows + start, 16), count)

    def remote(src, dst, ss, rs, to):
        return pltpu.make_async_remote_copy(
            src_ref=src, dst_ref=dst, send_sem=ss, recv_sem=rs,
            device_id={"solve": to}, device_id_type=MESH,
        )

    loads = [
        pltpu.make_async_copy(beliefs, beliefs_t, load_s.at[0]),
        pltpu.make_async_copy(targets, targets_t, load_s.at[1]),
    ]
    for load in loads:
        load.start()

    barrier = pltpu.get_barrier_semaphore()
    for to in (*zp[1:], xn, yn, sib):
        pl.semaphore_signal(barrier, inc=1, device_id={"solve": to}, device_id_type=MESH)
    pl.semaphore_wait(barrier, 6)

    started = []
    used = [0, 0]

    def gather_send(k, src_dev, to, part=None, own=None):
        w = (w1, w2)[k]
        span = (0, rows) if part is None else (part * half, half)
        place = w.at[block(src_dev, *span)]
        slot = used[k]
        used[k] += 1
        rsem = ag_r.at[k, src_dev] if part != 1 else ag_r.at[k, n + src_dev // 8]
        cp = remote(place if own is None else own, place, ag_s.at[k, slot], rsem, to)
        cp.start()
        started.append(cp)

    def gather_wait(k, src_dev, part=None):
        w = (w1, w2)[k]
        span = (0, rows) if part is None else (part * half, half)
        place = w.at[block(src_dev, *span)]
        rsem = ag_r.at[k, src_dev] if part != 1 else ag_r.at[k, n + src_dev // 8]
        remote(place, place, ag_s.at[k, 0], rsem, sib).wait_recv()

    for k, own in ((0, enc), (1, head)):
        for to in (zp[1], xn, yn, zp[2], zp[3], sib):
            gather_send(k, me, to, own=own)
    w1[block(me)] = enc[...]
    w2[block(me)] = head[...]

    def forward_column(k, q):
        src = dev(zs[q], y, x, c)
        gather_wait(k, src)
        for to in (sib,) if q == 1 else (xn, yn, sib):
            gather_send(k, src, to)

    def forward_plane(k, q):
        src = dev(zs[q], y, 1 - x, c)
        gather_wait(k, src)
        if q == 0:
            gather_send(k, src, zp[1])
        gather_send(k, src, yn, part=0)
        gather_send(k, src, sib)
        src = dev(zs[q], 1 - y, x, c)
        gather_wait(k, src)
        if q == 0:
            gather_send(k, src, zp[1])
        gather_send(k, src, xn, part=1)
        gather_send(k, src, sib)

    def forward_diagonal(k, q):
        src = dev(zs[q], 1 - y, 1 - x, c)
        gather_wait(k, src, 0)
        gather_wait(k, src, 1)
        gather_send(k, src, sib)

    def wait_sibling(k, dz):
        for yy in (0, 1):
            for xx in (0, 1):
                gather_wait(k, dev(zs[dz], yy, xx, 1 - c))

    forward_plane(0, 0)
    for q in (1, 2, 3):
        forward_column(0, q)
    forward_plane(1, 0)
    for q in (1, 2, 3):
        forward_column(1, q)
    for q in (1, 2, 3):
        forward_plane(0, q)
    for q in (1, 2, 3):
        forward_plane(1, q)

    card_onehot = (
        lax.broadcasted_iota(jnp.int32, (blockers.shape[0], leaves), 0) == card[...]
    ).astype(F32).T.astype(BF16)
    for start in range(0, width, 256):
        cols = slice(start, min(start + 256, width))
        opened[:, cols] = (
            1.0 - jnp.dot(card_onehot, blockers[:, cols], preferred_element_type=F32)
        ).astype(BF16)
    for q in range(4):
        forward_diagonal(0, q)

    for load in loads:
        load.wait()
    for q in range(4):
        wait_sibling(0, q)
        units = pl.ds(pl.multiple_of(zs[q] * plane, plane), plane)
        pre = jnp.dot(w1[units, :], beliefs_t[...], preferred_element_type=F32)
        act = pre / (1.0 + jnp.exp(-pre))
        hidden_t[units, :] = act.astype(BF16)
        hidden[:, units] = act.T.astype(BF16)
        forward_diagonal(1, q)
    for start in range(0, width, 256):
        cols = slice(start, min(start + 256, width))
        errors[:, cols] = targets_t[cols, :].astype(F32).T.astype(BF16)
    for q in range(4):
        wait_sibling(1, q)

    def output_columns(cols):
        out = jnp.dot(hidden[...], w2[:, cols], preferred_element_type=F32)
        errors[:, cols] = ((out - errors[:, cols].astype(F32)) * (1.0 / leaves)).astype(BF16)
        leaf[:, cols] = out.astype(BF16)

    full = width // 256

    def output_step(j, _):
        output_columns(pl.ds(pl.multiple_of(j * 256, 256), 256))
        return _

    lax.fori_loop(0, full, output_step, 0)
    if full * 256 < width:
        output_columns(slice(full * 256, width))

    order = (1, 2, 3, 0)
    pend = {}
    rs_used = [0]

    def reduce_send(name, src, dst, to):
        slot = rs_used[0]
        rs_used[0] += 1
        cp = remote(src, dst, rs_s.at[slot], rs_r.at[slot], to)
        cp.start()
        started.append(cp)
        pend[name] = cp

    def in_plane(yy, xx, cc):
        return pl.ds(pl.multiple_of((yy * 4 + xx * 2 + cc) * rows, rows), rows)

    rel = ((y, x), (y, 1 - x), (1 - y, x), (1 - y, 1 - x))

    def compute(p):
        units = pl.ds(pl.multiple_of(zs[order[p]] * plane, plane), plane)
        partial[p] = jnp.dot(hidden_t[units, :], errors[...], preferred_element_type=F32)
        for r in (3, 1, 2, 0):
            yy, xx = rel[r]
            sib_send[p, r] = partial[p, in_plane(yy, xx, 1 - c)].astype(BF16)
            reduce_send(("s", p, r), sib_send.at[p, r], sib_recv.at[p, r], sib)

    def chip_sum(p, r, lo=0, count=rows):
        yy, xx = rel[r]
        base = (yy * 4 + xx * 2 + c) * rows + lo
        own = partial[p, pl.ds(pl.multiple_of(base, 16), count)]
        return own + sib_recv[p, r, lo:lo + count].astype(F32)

    def stage_diagonal(p):
        pend["s", p, 3].wait_recv()
        diag_send[p] = chip_sum(p, 3).astype(BF16)
        reduce_send(("a", p), diag_send.at[p, pl.ds(0, half)], diag_recv.at[p, pl.ds(0, half)], yn)
        reduce_send(("b", p), diag_send.at[p, pl.ds(half, half)], diag_recv.at[p, pl.ds(half, half)], xn)

    def stage_neighbours(p):
        for r, name, to, lo in ((1, "a", xn, 0), (2, "b", yn, half)):
            pend["s", p, r].wait_recv()
            pend[name, p].wait_recv()
            total = chip_sum(p, r)
            there = diag_recv[p, lo:lo + half].astype(F32)
            keep = total[half - lo:half - lo + half]
            mixed = total[lo:lo + half] + there
            if p == 3:
                pend["n", 0, r].wait_recv()
                extra = xy_recv[0, r - 1].astype(F32)
                mixed += extra[lo:lo + half]
                keep += extra[half - lo:half - lo + half]
            xy_send[p, r - 1, lo:lo + half] = mixed.astype(BF16)
            xy_send[p, r - 1, half - lo:half - lo + half] = keep.astype(BF16)
            reduce_send(("n", p, r), xy_send.at[p, r - 1], xy_recv.at[p, r - 1], zp[1] if p == 0 else to)

    def column_sum(p):
        pend["s", p, 0].wait_recv()
        total = chip_sum(p, 0)
        if p > 0:
            for r in (1, 2):
                pend["n", p, r].wait_recv()
                total += xy_recv[p, r - 1].astype(F32)
        return total

    def stage_column(p):
        z_send[p] = column_sum(p).astype(BF16)
        reduce_send(("z", p), z_send.at[p], z_recv.at[p], zp[order[p]])

    small = {}
    small_used = [0]

    def small_send(name, src, dst, to):
        slot = small_used[0]
        small_used[0] += 1
        cp = remote(src, dst, small_s.at[slot], small_r.at[slot], to)
        cp.start()
        started.append(cp)
        small[name] = cp

    def flip(bit, by):
        return bit + by - 2 * bit * by

    def line_terms():
        r = lax.broadcasted_iota(jnp.int32, (n, leaves), 0)
        far = [lax.rem(r // 2 ** b, 2) for b in range(5)]
        owner = (
            16 * flip(z_high, far[1]) + 8 * flip(z_low, far[0])
            + 4 * flip(y, far[2]) + 2 * flip(x, far[3]) + flip(c, far[4])
        )
        onehot = (owner == line[...]).astype(F32).astype(BF16)
        for start in range(0, width, 512):
            cols = slice(start, min(start + 512, width))
            masked = (leaf[:, cols].astype(F32) * opened[:, cols].astype(F32)).astype(BF16)
            line_tree[:, cols] = jnp.dot(onehot, masked, preferred_element_type=F32) / open_turns
        small_send("lc", line_tree.at[pl.ds(16, 16)], line_in.at[pl.ds(16, 16)], sib)

    def line_x():
        small["lc"].wait_recv()
        line_tree[0:16] += line_in[16:32]
        small_send("lx", line_tree.at[pl.ds(8, 8)], line_in.at[pl.ds(8, 8)], xn)

    def line_y():
        small["lx"].wait_recv()
        both = line_tree[0:8] + line_in[8:16]
        line_tree[0:8] = both
        y_send[0:4] = both[4:8]
        small_send("ly", y_send, y_in, yn)

    def line_z():
        small["ly"].wait_recv()
        four = line_tree[0:4] + y_in[0:4]
        line_tree[0:4] = four
        for q in (1, 2, 3):
            lz_send[q - 1] = four[q:q + 1]
            small_send(("lz", q), lz_send.at[q - 1], lz_in.at[q - 1], zp[q])

    positive = jnp.maximum(regrets[...], 0.0) + regret_floor

    def line_done():
        value = line_tree[0:1]
        for q in (1, 2, 3):
            small["lz", q].wait_recv()
            value += lz_in[q - 1]
        line_values[...] = value
        sums[0, 0:1] = positive * value[:, :hands]
        sums[0, 1:2] = positive
        small_send("nc", sums.at[0], sums_in.at[0], sib)

    def sums_step(at, name, following, to):
        small[name].wait_recv()
        sums[at, 0:2] = sums[at - 1, 0:2] + sums_in[at - 1, 0:2]
        for q, dst in enumerate(to):
            small_send((following, q), sums.at[at], sums_in.at[at + q], dst)

    def root_done():
        total = sums[3, 0:2]
        for q in (0, 1, 2):
            small["nz", q].wait_recv()
            total += sums_in[3 + q, 0:2]
        root = total[0:1] / total[1:2]
        new_regrets[...] = regrets[...] + line_values[:, :hands] - root

    y_send[4:8] = jnp.zeros((4, width), F32)
    sums[...] = jnp.zeros_like(sums)
    compute(0)
    compute(1)
    line_terms()
    stage_diagonal(0)
    compute(2)
    line_x()
    stage_diagonal(1)
    stage_neighbours(0)
    line_y()
    compute(3)
    stage_diagonal(2)
    stage_neighbours(1)
    line_z()
    stage_column(0)
    stage_diagonal(3)
    line_done()
    stage_neighbours(2)
    sums_step(1, "nc", "nx", (xn,))
    stage_column(1)
    stage_neighbours(3)
    sums_step(2, ("nx", 0), "ny", (yn,))
    stage_column(2)
    sums_step(3, ("ny", 0), "nz", zp[1:])
    root_done()

    result = column_sum(3)
    for p in range(3):
        pend["z", p].wait_recv()
        result += z_recv[p].astype(F32)
    head_grad[...] = result

    for cp in started:
        cp.wait_send()

def fused(nz, beliefs, targets, leaf_line, turn_card, encoder, value_head, regrets):
    n = nz * 8
    leaves, width = beliefs.shape
    hands = regrets.shape[1]
    rows = value_head.shape[0]
    units = rows * n
    table = blocker_table(hands, 64)
    blockers = jnp.asarray(np.concatenate([table, table], 1), dtype=BF16)
    vm = pl.BlockSpec(memory_space=pltpu.VMEM)
    dma = pltpu.SemaphoreType.DMA
    outs = pl.pallas_call(
        functools.partial(step_kernel, nz, hands),
        out_shape=(
            jax.ShapeDtypeStruct((1, hands), F32),
            jax.ShapeDtypeStruct((1, width), F32),
            jax.ShapeDtypeStruct((rows, width), F32),
        ),
        in_specs=[pl.BlockSpec(memory_space=pl.ANY)] * 2 + [vm] * 6,
        out_specs=(vm, vm, vm),
        scratch_shapes=[
            pltpu.VMEM((width, leaves), BF16),
            pltpu.VMEM((width, leaves), BF16),
            pltpu.VMEM((units, width), BF16),
            pltpu.VMEM((units, width), BF16),
            pltpu.VMEM((leaves, width), BF16),
            pltpu.VMEM((leaves, width), BF16),
            pltpu.VMEM((leaves, width), BF16),
            pltpu.VMEM((leaves, units), BF16),
            pltpu.VMEM((units, leaves), BF16),
            pltpu.VMEM((4, rows * 8, width), F32),
            pltpu.VMEM((4, 4, rows, width), BF16),
            pltpu.VMEM((4, 4, rows, width), BF16),
            pltpu.VMEM((4, rows, width), BF16),
            pltpu.VMEM((4, rows, width), BF16),
            pltpu.VMEM((4, 2, rows, width), BF16),
            pltpu.VMEM((4, 2, rows, width), BF16),
            pltpu.VMEM((3, rows, width), BF16),
            pltpu.VMEM((3, rows, width), BF16),
            pltpu.VMEM((n, width), F32),
            pltpu.VMEM((n, width), F32),
            pltpu.VMEM((8, width), F32),
            pltpu.VMEM((8, width), F32),
            pltpu.VMEM((3, 1, width), F32),
            pltpu.VMEM((3, 1, width), F32),
            pltpu.VMEM((4, 8, hands), F32),
            pltpu.VMEM((6, 8, hands), F32),
            dma((2, 40)),
            dma((2, n + nz)),
            dma((40,)),
            dma((40,)),
            dma((16,)),
            dma((16,)),
            dma((2,)),
        ],
        compiler_params=pltpu.CompilerParams(
            collective_id=0, has_side_effects=True, vmem_limit_bytes=62 * 2**20
        ),
        cost_estimate=pl.CostEstimate(
            flops=6 * leaves * width * units, bytes_accessed=12 * 2**20, transcendentals=leaves * units
        ),
    )(
        beliefs.T, targets.T, leaf_line.reshape(1, leaves), turn_card.reshape(1, leaves),
        encoder.T, value_head, regrets, blockers,
    )
    return pl.pallas_call(
        hand_over, out_shape=tuple(jax.ShapeDtypeStruct(o.shape, o.dtype) for o in outs), in_specs=[vm] * 3, out_specs=(vm, vm, vm)
    )(*outs)


def hand_over(a, b, c, a_out, b_out, c_out):
    a_out[...] = a[...]
    b_out[...] = b[...]
    c_out[...] = c[...]


def by_collectives(beliefs, targets, leaf_line, turn_card, encoder, value_head, regrets):
    devices = lax.axis_size("solve")
    leaf_count = beliefs.shape[0]
    hand_count = regrets.shape[1]
    line_count = regrets.shape[0] * devices
    hidden = jax.nn.silu(
        jnp.dot(
            beliefs,
            lax.all_gather(encoder, "solve", axis=1, tiled=True),
            preferred_element_type=F32,
        )
    ).astype(BF16)
    output = jnp.dot(
        hidden,
        lax.all_gather(value_head, "solve", axis=0, tiled=True),
        preferred_element_type=F32,
    )
    errors = ((output - targets.astype(F32)) / leaf_count).astype(BF16)
    head_grad = lax.psum_scatter(
        lax.dot_general(hidden, errors, (((0,), (0,)), ((), ())), preferred_element_type=F32),
        "solve", scatter_dimension=0, tiled=True,
    )
    card_onehot = (turn_card[:, None] == jnp.arange(52, dtype=jnp.int32)[None, :]).astype(BF16)
    blocked = jnp.dot(
        card_onehot, jnp.asarray(blocker_table(hand_count), dtype=BF16), preferred_element_type=F32
    )
    shown = (1.0 - blocked).astype(BF16)
    weighted = output.astype(BF16) * jnp.concatenate([shown, shown], 1)
    line_onehot = (leaf_line[:, None] == jnp.arange(line_count, dtype=jnp.int32)[None, :]).astype(BF16)
    line_values = lax.psum_scatter(
        lax.dot_general(
            line_onehot, weighted, (((0,), (0,)), ((), ())), preferred_element_type=F32
        ) / open_turns,
        "solve", scatter_dimension=0, tiled=True,
    )
    positive = jnp.maximum(regrets, 0.0) + regret_floor
    denominator, numerator = lax.psum(
        (jnp.sum(positive, 0), jnp.sum(positive * line_values[:, :hand_count], 0)), "solve"
    )
    new_regrets = regrets + line_values[:, :hand_count] - (numerator / denominator)[None, :]
    return (new_regrets, line_values, head_grad)


def solution(mesh):
    split = P(("groups", "solve"), None)
    placed = (
        split, split, P(("groups", "solve")), P(("groups", "solve")),
        P(None, "solve"), P("solve", None), split,
    )
    in_tree = mesh.shape["groups"] == 1 and mesh.shape["solve"] == 32
    return jax.shard_map(
        functools.partial(fused, mesh.shape["solve"] // 8) if in_tree else by_collectives,
        mesh=mesh,
        in_specs=placed,
        out_specs=(split, split, split),
        check_vma=False,
    )
```
